256 devices in a mesh: row: 16 (over z, core), col: 16 (over y, x).
Axes of the slice: x: 4, y: 4, z: 8, core: 2. Of those that a mesh axis runs over, the one named last changes fastest.
Arguments:
- momentum: float32 [8192, 26624], P('row', 'col'), may hold values from -20 to 20
- grad: bfloat16 [8192, 26624], P('row', 'col'), may hold values from -3 to 3
- basis: float32 [26624, 128], P('col'), may hold values from -0.0390625 to 0.0390625
Outputs:
- momentum_out: float32 [8192, 26624], P('row', 'col')
- left_out: float32 [2, 8192, 128], P(None, 'row')
- right_out: float32 [26624, 128], P('col')
The draws below stay inside these ranges and needn't reach their ends.
All inputs are finite; a program needn't handle non-finite values.
Results may differ from the reference program's by a relative error of at most 0.0003.
Values sent between devices are 32-bit elements; how exact they have to be, the bound alone decides.
A program may use at most 64 MiB of HBM per device.

```python
import jax
import jax.numpy as jnp
from jax import lax

RANK = 128
ITERS = 2
ROWS = 8192
COLS = 26624


def draw_momentum(key, part):
    key = jax.random.fold_in(key, 7)
    keys = jax.random.split(key, 3)
    row_pos = jnp.arange(ROWS, dtype=jnp.float32) / ROWS
    col_pos = jnp.arange(COLS, dtype=jnp.float32) / COLS
    row_scale = jnp.exp(jnp.log(3.0) * row_pos) * jnp.exp(jax.random.uniform(keys[0], (ROWS,)) * jnp.log(4.0))
    col_scale = jnp.exp(jnp.log(3.0) * col_pos) * jnp.exp(jax.random.uniform(keys[1], (COLS,)) * jnp.log(4.0))
    base = jnp.clip(jax.random.normal(keys[2], (ROWS, COLS)), -4.0, 4.0)
    values = 0.3 * base * row_scale[:, None] * col_scale[None, :]
    return jnp.clip(values, -20.0, 20.0).astype(jnp.float32)


def levels(own_key, dims, cuts, least, largest):
    factor_of = 1.0
    for dim, shards_of in cuts:
        steps = jax.random.uniform(jax.random.fold_in(jax.random.fold_in(own_key, 6), dim), (shards_of,), jnp.float32, least / len(cuts), largest / len(cuts))
        factor_of = factor_of * jnp.repeat(jnp.exp(steps), dims[dim] // shards_of).reshape((-1,) + (1,) * (len(dims) - 1 - dim))
    return factor_of


def noise(stream_key, dims, width, most, cuts=(), held_as=jnp.bfloat16):
    gain = levels(stream_key, dims, cuts, -0.22, 0.18) if cuts else 1.0
    drawn = jax.random.normal(stream_key, dims, jnp.float32) * width * gain
    return jnp.minimum(jnp.maximum(drawn, -most), most).astype(held_as)


def setup_inputs(seed: int = 0) -> dict:
    seeds = jax.random.split(jax.random.key(seed), 4)
    momentum = draw_momentum(jax.random.fold_in(seeds[3], 71), 0)
    grad = noise(seeds[1], (ROWS, COLS), 0.5, 3.0, ((0, 16), (1, 16)))
    basis = noise(seeds[2], (COLS, RANK), COLS ** -0.5, 0.0390625, ((0, 16),), jnp.float32)
    return {"momentum": momentum, "grad": grad, "basis": basis}


def orthonormal(proj):
    gram = jnp.dot(proj.T, proj, precision=lax.Precision.HIGHEST)
    lower = jnp.linalg.cholesky(gram)
    return jax.scipy.linalg.solve_triangular(lower, proj.T, lower=True).T

def reference(momentum, grad, basis):
    work = momentum + grad.astype(jnp.float32)
    lefts = []
    for step in range(ITERS):
        proj = jnp.dot(work, basis, precision=lax.Precision.HIGHEST)
        left = orthonormal(proj)
        right_raw = jnp.dot(work.T, left, precision=lax.Precision.HIGHEST)
        basis = orthonormal(right_raw)
        work = work - 0.95 * jnp.dot(left, right_raw.T, precision=lax.Precision.HIGHEST)
        lefts.append(left * jnp.sqrt(jnp.float32(ROWS)))
    return (work, jnp.stack(lefts), basis * jnp.sqrt(jnp.float32(COLS)))
```

```python
import functools
import math

import jax
import jax.numpy as jnp
from jax import lax
from jax.experimental import pallas as pl
from jax.experimental.pallas import tpu as pltpu
from jax.sharding import PartitionSpec as P

RANK = 128
MESH = pl.DeviceIdType.MESH
HIGHEST = lax.Precision.HIGHEST
F32 = jnp.float32
BF16 = jnp.bfloat16
NN = (((1,), (0,)), ((), ()))
NT = (((1,), (1,)), ((), ()))
TN = (((0,), (0,)), ((), ()))


def dot(a, b, dims=NN):
    return lax.dot_general(a, b, dims, preferred_element_type=F32)


def exact(a, b, dims=NN):
    return lax.dot_general(a, b, dims, precision=HIGHEST, preferred_element_type=F32)


def split(x):
    high = x.astype(BF16)
    return high, (x - high.astype(F32)).astype(BF16)


def tiles(total, size):
    return [(i, min(size, total - i)) for i in range(0, total, size)]


def inverse_cholesky(a_ref):
    lane = lax.broadcasted_iota(jnp.int32, (8, RANK), 1)
    sub = lax.broadcasted_iota(jnp.int32, (8, RANK), 0)
    row_all = lax.broadcasted_iota(jnp.int32, (RANK, RANK), 0)
    lane_all = lax.broadcasted_iota(jnp.int32, (RANK, RANK), 1)

    def panel(k, carry):
        o = pl.multiple_of(k * 8, 8)
        v = a_ref[pl.ds(o, 8), :]
        front = pltpu.roll(v, lax.rem(RANK - o, RANK), 1)
        cols = [jnp.broadcast_to(front[:, j : j + 1], (8, RANK)) for j in range(8)]
        inside = (lane >= o) & (lane < o + 8)
        v = jnp.where(inside, jnp.where(lane == o + sub, 1.0, 0.0), v)
        for j in range(8):
            d = jnp.broadcast_to(cols[j][j : j + 1, :], (8, RANK))
            r = lax.rsqrt(d)
            r = r * (1.5 - 0.5 * d * r * r)
            m = jnp.where(sub > j, cols[j] * r, 0.0)
            scaled = jnp.broadcast_to(v[j : j + 1, :], (8, RANK)) * r
            v = jnp.where(sub == j, scaled, v - m * scaled)
            for l in range(j + 1, 8):
                e = jnp.broadcast_to(cols[l][j : j + 1, :], (8, RANK)) * r
                cols[l] = cols[l] - m * e
        behind = jnp.where(lane >= o + 8, v, 0.0)
        update = exact(behind, v, TN)
        old = a_ref[...]
        clear = (row_all >= o + 8) & (lane_all >= o) & (lane_all < o + 8)
        a_ref[...] = jnp.where(clear, 0.0, old) - update
        a_ref[pl.ds(o, 8), :] = jnp.where(lane < o + 8, v, 0.0)
        return carry

    lax.fori_loop(0, RANK // 8, panel, 0)


def kernel(
    n_col, n_z, mom_ref, grad_ref, basis_ref, mom_out, left_out, right_out,
    w, wh, wl, b2, proj, pt2, rt, rt2, left, gram,
    c_src, c_rs, c_own, c_ag, st, r_half, r_sum, r_rs, r_own, r_ag, sx, g_src, g_rs, g_own, g_ag,
    send, recv,
):
    rows, cols = mom_ref.shape
    row = lax.axis_index("row")
    me = lax.axis_index("col")
    z = row // 2
    core = lax.rem(row, 2)
    total_rows = rows * 2 * n_z
    total_cols = cols * n_col
    at_col = lambda p: (row, p)
    at_z = lambda p: (p * 2 + core, me)
    partner = (z * 2 + 1 - core, me)

    barrier = pltpu.get_barrier_semaphore()

    def greet_col(s, carry):
        pl.semaphore_signal(barrier, inc=1, device_id=at_col(lax.rem(me + s, n_col)), device_id_type=MESH)
        return carry

    def greet_z(s, carry):
        pl.semaphore_signal(barrier, inc=1, device_id=at_z(lax.rem(z + s, n_z)), device_id_type=MESH)
        return carry

    lax.fori_loop(1, n_col, greet_col, 0)
    lax.fori_loop(1, n_z, greet_z, 0)
    pl.semaphore_signal(barrier, inc=1, device_id=partner, device_id_type=MESH)
    pl.semaphore_wait(barrier, n_col + n_z - 1)

    def remote(src, dst, sem, to):
        return pltpu.make_async_remote_copy(
            src_ref=src, dst_ref=dst, send_sem=send.at[sem], recv_sem=recv.at[sem],
            device_id=to, device_id_type=MESH,
        )

    def reduce_all(n, mine, at, src, rs, own, ag, put, sem):
        def spread(s, carry):
            p = lax.rem(mine + s, n)
            remote(src.at[p], rs.at[s - 1], sem, at(p)).start()
            return carry

        lax.fori_loop(1, n, spread, 0)
        remote(rs, rs, sem, at(mine)).wait_recv()
        total = src[mine]
        for s in range(n - 1):
            total = total + rs[s]
        own[...] = total

        def gather(s, carry):
            p = lax.rem(mine + s, n)
            remote(own, ag.at[s - 1], sem + 1, at(p)).start()
            return carry

        lax.fori_loop(1, n, gather, 0)
        put(mine, total)
        remote(ag, ag, sem + 1, at(mine)).wait_recv()
        for s in range(1, n):
            put(lax.rem(mine - s + n, n), ag[s - 1])
        remote(rs, rs, sem, at(mine)).wait_send()
        remote(ag, ag, sem + 1, at(mine)).wait_send()

    def reduce_rows(sem):
        away = pl.ds(pl.multiple_of((1 - core) * n_z, n_z), n_z)
        home = pl.ds(pl.multiple_of(core * n_z, n_z), n_z)
        first = remote(st.at[away], r_half, sem, partner)
        first.start()
        first.wait()
        r_sum[...] = st[home] + r_half[...]

        def put(q, value):
            sx[core * n_z + q] = value

        reduce_all(n_z, z, at_z, r_sum, r_rs, r_own, r_ag, put, sem + 1)
        last = remote(sx.at[home], sx.at[home], sem + 3, partner)
        last.start()
        last.wait()

    def transposed_products():
        pt = proj[...].T
        h, l = split(pt)
        pt2[pl.ds(0, RANK), :] = h
        pt2[pl.ds(RANK, RANK), :] = l
        st[:, :, pl.ds(cols, RANK)] = exact(pt, pt, NT).reshape(2 * n_z, 8, RANK)
        for o, size in tiles(cols, 256):
            a = dot(pt2[...], wh[:, pl.ds(o, size)]) + dot(pt2[...], wl[:, pl.ds(o, size)])
            st[:, :, pl.ds(o, size)] = (a[:RANK] + a[RANK:]).reshape(2 * n_z, 8, size)

    def right_raw():
        gram[...] = sx[:, :, pl.ds(cols, RANK)].reshape(RANK, RANK)
        inverse_cholesky(gram)
        for o, size in tiles(cols, 256):
            value = exact(gram[...], sx[:, :, pl.ds(o, size)].reshape(RANK, size))
            rt[:, pl.ds(o, size)] = value
            h, l = split(value)
            rt2[pl.ds(0, RANK), pl.ds(o, size)] = h
            rt2[pl.ds(RANK, RANK), pl.ds(o, size)] = l
        return exact(rt[...], rt[...], NT)

    def set_left(index):
        for o, size in tiles(rows, 128):
            value = exact(proj[pl.ds(o, size), :], gram[...], NT)
            left[pl.ds(o, size), :] = value
            left_out[index, pl.ds(o, size), :] = value * F32(math.sqrt(total_rows))

    def deflate(write):
        for o, size in tiles(rows, 128):
            h, l = split(left[pl.ds(o, size), :])
            hl = jnp.concatenate([h, l], axis=1)
            lh = jnp.concatenate([l, h], axis=1)
            for p, width in tiles(cols, 256):
                outer = dot(hl, rt2[:, pl.ds(p, width)]) + dot(lh, rt2[:, pl.ds(p, width)])
                write(o, size, p, width, w[pl.ds(o, size), pl.ds(p, width)] - 0.95 * outer)

    h, l = split(basis_ref[...])
    b2[:, pl.ds(0, RANK)] = h
    b2[:, pl.ds(RANK, RANK)] = l
    per = rows // n_col

    def set_work(o, size, p, width, value):
        w[pl.ds(o, size), pl.ds(p, width)] = value
        h, l = split(value)
        wh[pl.ds(o, size), pl.ds(p, width)] = h
        wl[pl.ds(o, size), pl.ds(p, width)] = l

    for o, size in tiles(rows, 128):
        for p, width in tiles(cols, 256):
            value = mom_ref[pl.ds(o, size), pl.ds(p, width)] + grad_ref[pl.ds(o, size), pl.ds(p, width)].astype(F32)
            set_work(o, size, p, width, value)
        a = dot(wh[pl.ds(o, size), :], b2[...]) + dot(wl[pl.ds(o, size), :], b2[...])
        c_src[pl.ds(o // per, size // per), pl.ds(0, per), :] = (a[:, :RANK] + a[:, RANK:]).reshape(size // per, per, RANK)
    c_src[:, pl.ds(per, 8), :] = jnp.zeros((n_col, 8, RANK), F32)

    def put_proj(q, value):
        proj[pl.ds(pl.multiple_of(q * per, per), per), :] = value[:per]
        gram[pl.ds(pl.multiple_of(q * 8, 8), 8), :] = value[per:]

    reduce_all(n_col, me, at_col, c_src, c_rs, c_own, c_ag, put_proj, 0)
    transposed_products()
    reduce_rows(2)
    gram_part = right_raw()
    for o, size in tiles(rows, 128):
        a = dot(wh[pl.ds(o, size), :], rt2[...], NT) + dot(wl[pl.ds(o, size), :], rt2[...], NT)
        c_src[pl.ds(o // per, size // per), pl.ds(0, per), :] = (a[:, :RANK] + a[:, RANK:]).reshape(size // per, per, RANK)
    c_src[:, pl.ds(per, 8), :] = gram_part.reshape(n_col, 8, RANK)
    set_left(0)
    deflate(set_work)
    reduce_all(n_col, me, at_col, c_src, c_rs, c_own, c_ag, put_proj, 6)
    full_gram = gram[...]
    inverse_cholesky(gram)
    for o, size in tiles(rows, 128):
        value = proj[pl.ds(o, size), :] - 0.95 * exact(left[pl.ds(o, size), :], full_gram)
        proj[pl.ds(o, size), :] = exact(value, gram[...], NT)
    transposed_products()
    reduce_rows(8)
    gram_part = right_raw()
    set_left(1)

    def set_out(o, size, p, width, value):
        mom_out[pl.ds(o, size), pl.ds(p, width)] = value

    deflate(set_out)
    g_src[...] = gram_part.reshape(n_col, 8, RANK)

    def put_gram(q, value):
        gram[pl.ds(pl.multiple_of(q * 8, 8), 8), :] = value

    reduce_all(n_col, me, at_col, g_src, g_rs, g_own, g_ag, put_gram, 12)
    inverse_cholesky(gram)
    for o, size in tiles(cols, 128):
        value = exact(gram[...], rt[:, pl.ds(o, size)]) * F32(math.sqrt(total_cols))
        right_out[pl.ds(o, size), :] = value.T


def shards(momentum, grad, basis):
    rows, cols = momentum.shape
    n_col = lax.axis_size("col")
    n_z = lax.axis_size("row") // 2
    per = rows // n_col
    wide = cols + RANK
    vmem = pl.BlockSpec(memory_space=pltpu.VMEM)
    scratch = [
        ((rows, cols), F32), ((rows, cols), BF16), ((rows, cols), BF16), ((cols, 2 * RANK), BF16),
        ((rows, RANK), F32), ((2 * RANK, rows), BF16), ((RANK, cols), F32), ((2 * RANK, cols), BF16),
        ((rows, RANK), F32), ((RANK, RANK), F32),
        ((n_col, per + 8, RANK), F32), ((n_col - 1, per + 8, RANK), F32), ((per + 8, RANK), F32), ((n_col - 1, per + 8, RANK), F32),
        ((2 * n_z, 8, wide), F32), ((n_z, 8, wide), F32), ((n_z, 8, wide), F32), ((n_z - 1, 8, wide), F32),
        ((8, wide), F32), ((n_z - 1, 8, wide), F32), ((2 * n_z, 8, wide), F32),
        ((n_col, 8, RANK), F32), ((n_col - 1, 8, RANK), F32), ((8, RANK), F32), ((n_col - 1, 8, RANK), F32),
    ]
    return pl.pallas_call(
        functools.partial(kernel, n_col, n_z),
        out_shape=(
            jax.ShapeDtypeStruct((rows, cols), F32),
            jax.ShapeDtypeStruct((2, rows, RANK), F32),
            jax.ShapeDtypeStruct((cols, RANK), F32),
        ),
        in_specs=[vmem] * 3,
        out_specs=(vmem,) * 3,
        scratch_shapes=[pltpu.VMEM(s, t) for s, t in scratch]
        + [pltpu.SemaphoreType.DMA((14,)), pltpu.SemaphoreType.DMA((14,))],
        compiler_params=pltpu.CompilerParams(
            collective_id=0, has_side_effects=True, vmem_limit_bytes=56 * 1024 * 1024
        ),
    )(momentum, grad, basis)


def solution(mesh):
    in_specs = (P("row", "col"), P("row", "col"), P("col", None))
    out_specs = (P("row", "col"), P(None, "row", None), P("col", None))
    return jax.shard_map(shards, mesh=mesh, in_specs=in_specs, out_specs=out_specs, check_vma=False)
```

```python
import functools
import math

import jax
import jax.numpy as jnp
from jax import lax
from jax.experimental import pallas as pl
from jax.experimental.pallas import tpu as pltpu
from jax.sharding import PartitionSpec as P

RANK = 128
TILE = 128
PIECES = 4
MESH = pl.DeviceIdType.MESH
HIGHEST = lax.Precision.HIGHEST
F32 = jnp.float32
BF16 = jnp.bfloat16
NN = (((1,), (0,)), ((), ()))
NT = (((1,), (1,)), ((), ()))
TN = (((0,), (0,)), ((), ()))


def dot(a, b, dims=NN):
    return lax.dot_general(a, b, dims, preferred_element_type=F32)


def exact(a, b, dims=NN):
    return lax.dot_general(a, b, dims, precision=HIGHEST, preferred_element_type=F32)


def split(x):
    high = x.astype(BF16)
    return high, (x - high.astype(F32)).astype(BF16)


def fold(a):
    return a[:, :RANK] + a[:, RANK:]


def tiles(total, size):
    return [(i, min(size, total - i)) for i in range(0, total, size)]


def pieces_of(cols):
    blocks = cols // 128
    edges = [blocks * i // PIECES * 128 for i in range(PIECES + 1)]
    return [(a, b - a) for a, b in zip(edges[:-1], edges[1:])]


def inverse_cholesky(a_ref, first=0, last=RANK // 8):
    lane = lax.broadcasted_iota(jnp.int32, (8, RANK), 1)
    sub = lax.broadcasted_iota(jnp.int32, (8, RANK), 0)
    row_all = lax.broadcasted_iota(jnp.int32, (RANK, RANK), 0)
    lane_all = lax.broadcasted_iota(jnp.int32, (RANK, RANK), 1)

    def panel(k, carry):
        o = pl.multiple_of(k * 8, 8)
        v = a_ref[pl.ds(o, 8), :]
        front = pltpu.roll(v, lax.rem(RANK - o, RANK), 1)
        cols = [jnp.broadcast_to(front[:, j : j + 1], (8, RANK)) for j in range(8)]
        inside = (lane >= o) & (lane < o + 8)
        v = jnp.where(inside, jnp.where(lane == o + sub, 1.0, 0.0), v)
        for j in range(8):
            d = jnp.broadcast_to(cols[j][j : j + 1, :], (8, RANK))
            r = lax.rsqrt(d)
            r = r * (1.5 - 0.5 * d * r * r)
            m = jnp.where(sub > j, cols[j] * r, 0.0)
            scaled = jnp.broadcast_to(v[j : j + 1, :], (8, RANK)) * r
            v = jnp.where(sub == j, scaled, v - m * scaled)
            for l in range(j + 1, 8):
                e = jnp.broadcast_to(cols[l][j : j + 1, :], (8, RANK)) * r
                cols[l] = cols[l] - m * e
        behind = jnp.where(lane >= o + 8, v, 0.0)
        update = exact(behind, v, TN)
        old = a_ref[...]
        clear = (row_all >= o + 8) & (lane_all >= o) & (lane_all < o + 8)
        a_ref[...] = jnp.where(clear, 0.0, old) - update
        a_ref[pl.ds(o, 8), :] = jnp.where(lane < o + 8, v, 0.0)
        return carry

    lax.fori_loop(first, last, panel, 0)


def kernel(
    n_col, n_z, mom_ref, grad_ref, basis_ref, mom_out, left_out, right_out,
    w, grads, base, wh, wl, b2, proj, pt2, rt, rt2, left, gram, full_gram, acc, left_buf, right_buf,
    c_src, c_rs, c_all, g_src, g_rs, g_all, h_src, h_rs, h_all,
    io, send, recv, *piece_refs,
):
    rows, cols = w.shape
    pieces = pieces_of(cols)
    parts = [piece_refs[i * 5 : i * 5 + 5] for i in range(PIECES)]
    row = lax.axis_index("row")
    me = lax.axis_index("col")
    z = row // 2
    core = lax.rem(row, 2)
    n_row = 2 * n_z
    total_rows = rows * n_row
    total_cols = cols * n_col
    per = rows // n_col
    at_col = lambda p: (row, p)
    at_row = lambda p: (p, me)
    at_z = lambda p: (p * 2 + core, me)
    partner = (z * 2 + 1 - core, me)
    home = pl.ds(pl.multiple_of(core * n_z, n_z), n_z)
    away = pl.ds(pl.multiple_of((1 - core) * n_z, n_z), n_z)
    row_tiles = tiles(rows, TILE)

    barrier = pltpu.get_barrier_semaphore()

    def greet_col(s, carry):
        pl.semaphore_signal(barrier, inc=1, device_id=at_col(lax.rem(me + s, n_col)), device_id_type=MESH)
        return carry

    def greet_row(s, carry):
        pl.semaphore_signal(barrier, inc=1, device_id=at_row(lax.rem(row + s, n_row)), device_id_type=MESH)
        return carry

    lax.fori_loop(1, n_col, greet_col, 0)
    lax.fori_loop(1, n_row, greet_row, 0)

    loads = [pltpu.make_async_copy(basis_ref, base, io.at[0])]
    for i, (o, size) in enumerate(row_tiles):
        loads.append(pltpu.make_async_copy(mom_ref.at[pl.ds(o, size), :], w.at[pl.ds(o, size), :], io.at[1 + 2 * i]))
        loads.append(pltpu.make_async_copy(grad_ref.at[pl.ds(o, size), :], grads.at[pl.ds(o, size), :], io.at[2 + 2 * i]))
    for load in loads:
        load.start()

    def remote(src, dst, sem, to):
        return pltpu.make_async_remote_copy(
            src_ref=src, dst_ref=dst, send_sem=send.at[sem], recv_sem=recv.at[sem],
            device_id=to, device_id_type=MESH,
        )

    def scatter(n, mine, at, src, rs, sem):
        def one(s, carry):
            p = lax.rem(mine + s, n)
            remote(src.at[p], rs.at[s - 1], sem, at(p)).start()
            return carry

        lax.fori_loop(1, n, one, 0)

    def gather(n, mine, at, src, rs, full, base_slot, sem):
        remote(rs, rs, sem, partner).wait_recv()
        total = src[mine]
        for s in range(n - 1):
            total = total + rs[s]
        slot = base_slot + mine
        full[slot] = total

        def one(s, carry):
            p = lax.rem(mine + s, n)
            remote(full.at[slot], full.at[slot], sem + 1, at(p)).start()
            return carry

        lax.fori_loop(1, n, one, 0)

    def finish(rs, sem):
        remote(rs, rs, sem + 1, partner).wait_recv()
        remote(rs, rs, sem, partner).wait_send()
        remote(rs, rs, sem + 1, partner).wait_send()

    piece_sem = lambda i: 6 + 4 * i

    def column_start(i, o, size, a):
        first, count = o // per, size // per
        c_src[pl.ds(first, count)] = a.reshape(count, per, RANK)
        for q in range(first, first + count):
            @pl.when(q != me)
            def _():
                s = lax.rem(q - me + n_col, n_col)
                remote(c_src.at[q], c_rs.at[s - 1], 0, at_col(q)).start()

    def row_sums():
        pt = proj[...].T
        h, l = split(pt)
        pt2[pl.ds(0, RANK), :] = h
        pt2[pl.ds(RANK, RANK), :] = l
        g_src[...] = exact(pt, pt, NT).reshape(n_row, 8, RANK)
        scatter(n_row, row, at_row, g_src, g_rs, 4)
        swaps = []

        def onward(i):
            st, half, total, rs, sx = parts[i]
            swaps[i].wait()
            total[...] = st[home] + half[...]
            scatter(n_z, z, at_z, total, rs, piece_sem(i) + 1)

        for i, (o, size) in enumerate(pieces):
            st, half, total, rs, sx = parts[i]
            a = dot(pt2[...], wh[:, pl.ds(o, size)]) + dot(pt2[...], wl[:, pl.ds(o, size)])
            st[...] = (a[:RANK] + a[RANK:]).reshape(n_row, 8, size)
            swap = remote(st.at[away], half, piece_sem(i), partner)
            swap.start()
            swaps.append(swap)
            if i:
                onward(i - 1)
        onward(PIECES - 1)

        def gather_piece(i):
            st, half, total, rs, sx = parts[i]
            gather(n_z, z, at_z, total, rs, sx, core * n_z, piece_sem(i) + 1)

        backs = []

        def give_back(i):
            st, half, total, rs, sx = parts[i]
            finish(rs, piece_sem(i) + 1)
            back = remote(sx.at[home], sx.at[home], piece_sem(i) + 3, partner)
            back.start()
            backs.append(back)

        gather(n_row, row, at_row, g_src, g_rs, g_all, 0, 4)
        gather_piece(0)
        gather_piece(1)
        finish(g_rs, 4)
        gram[...] = g_all[...].reshape(RANK, RANK)
        inverse_cholesky(gram, 0, 2)
        gather_piece(2)
        inverse_cholesky(gram, 2, 5)
        gather_piece(3)
        inverse_cholesky(gram, 5, 10)
        give_back(0)
        inverse_cholesky(gram, 10, 13)
        give_back(1)
        inverse_cholesky(gram, 13, 16)
        give_back(2)
        return backs, give_back

    def right_raw(backs, give_back, with_product):
        part = None
        for i, (o, size) in enumerate(pieces):
            if i == PIECES - 1:
                give_back(i)
            backs[i].wait()
            sx = parts[i][4]
            value = exact(gram[...], sx[...].reshape(RANK, size))
            rt[:, pl.ds(o, size)] = value
            h, l = split(value)
            rt2[pl.ds(0, RANK), pl.ds(o, size)] = h
            rt2[pl.ds(RANK, RANK), pl.ds(o, size)] = l
            mine = exact(value, value, NT)
            part = mine if part is None else part + mine
            if i == PIECES - 1:
                h_src[...] = part.reshape(n_col, 8, RANK)
                scatter(n_col, me, at_col, h_src, h_rs, 2)
            if with_product:
                for k, (q, height) in enumerate(row_tiles):
                    here = pl.ds(q, height)
                    wide = rt2[:, pl.ds(o, size)]
                    a = dot(wh[here, pl.ds(o, size)], wide, NT) + dot(wl[here, pl.ds(o, size)], wide, NT)
                    if i:
                        a = a + acc[here, :]
                    if i < PIECES - 1:
                        acc[here, :] = a
                    else:
                        column_start(k, q, height, fold(a))

    def set_left(index):
        for o, size in row_tiles:
            value = exact(proj[pl.ds(o, size), :], gram[...], NT)
            left[pl.ds(o, size), :] = value
            left_buf[index, pl.ds(o, size), :] = value * F32(math.sqrt(total_rows))
        copy = pltpu.make_async_copy(left_buf.at[index], left_out.at[index], io.at[9 + index])
        copy.start()
        return copy

    def deflate(o, size, again):
        h, l = split(left[pl.ds(o, size), :])
        hl = jnp.concatenate([h, l], axis=1)
        lh = jnp.concatenate([l, h], axis=1)
        for p, width in tiles(cols, 256):
            outer = dot(hl, rt2[:, pl.ds(p, width)]) + dot(lh, rt2[:, pl.ds(p, width)])
            value = w[pl.ds(o, size), pl.ds(p, width)] - 0.95 * outer
            w[pl.ds(o, size), pl.ds(p, width)] = value
            if again:
                h, l = split(value)
                wh[pl.ds(o, size), pl.ds(p, width)] = h
                wl[pl.ds(o, size), pl.ds(p, width)] = l

    loads[0].wait()
    h, l = split(base[...])
    b2[:, pl.ds(0, RANK)] = h
    b2[:, pl.ds(RANK, RANK)] = l
    for i, (o, size) in enumerate(row_tiles):
        here = pl.ds(o, size)
        loads[1 + 2 * i].wait()
        loads[2 + 2 * i].wait()
        for p, width in tiles(cols, 256):
            value = w[here, pl.ds(p, width)] + grads[here, pl.ds(p, width)].astype(F32)
            w[here, pl.ds(p, width)] = value
            h, l = split(value)
            wh[here, pl.ds(p, width)] = h
            wl[here, pl.ds(p, width)] = l
        a = fold(dot(wh[here, :], b2[...]) + dot(wl[here, :], b2[...]))
        if i == 0:
            pl.semaphore_wait(barrier, n_col + n_row - 2)
        column_start(i, o, size, a)
    gather(n_col, me, at_col, c_src, c_rs, c_all, 0, 0)
    finish(c_rs, 0)
    proj[...] = c_all[...].reshape(rows, RANK)

    right_raw(*row_sums(), True)
    left_copies = [set_left(0)]
    deflate(*row_tiles[0], True)
    gather(n_col, me, at_col, h_src, h_rs, h_all, 0, 2)
    deflate(*row_tiles[1], True)
    gather(n_col, me, at_col, c_src, c_rs, c_all, 0, 0)
    for o, size in row_tiles[2:]:
        deflate(o, size, True)
    finish(h_rs, 2)
    full_gram[...] = h_all[...].reshape(RANK, RANK)
    gram[...] = full_gram[...]
    inverse_cholesky(gram)
    finish(c_rs, 0)
    for o, size in row_tiles:
        here = pl.ds(o, size)
        value = c_all[pl.ds(o // per, size // per)].reshape(size, RANK) - 0.95 * exact(left[here, :], full_gram[...])
        proj[here, :] = exact(value, gram[...], NT)

    right_raw(*row_sums(), False)
    left_copies.append(set_left(1))
    out_copies = []

    def finish_tile(i):
        o, size = row_tiles[i]
        deflate(o, size, False)
        copy = pltpu.make_async_copy(w.at[pl.ds(o, size), :], mom_out.at[pl.ds(o, size), :], io.at[11 + i])
        copy.start()
        out_copies.append(copy)

    for i in range(2):
        finish_tile(i)
    gather(n_col, me, at_col, h_src, h_rs, h_all, 0, 2)
    for i in range(2, len(row_tiles)):
        finish_tile(i)
    finish(h_rs, 2)
    gram[...] = h_all[...].reshape(RANK, RANK)
    inverse_cholesky(gram)
    for o, size in tiles(cols, 128):
        value = exact(gram[...], rt[:, pl.ds(o, size)]) * F32(math.sqrt(total_cols))
        right_buf[pl.ds(o, size), :] = value.T
    copy = pltpu.make_async_copy(right_buf, right_out, io.at[0])
    copy.start()
    for done in left_copies + out_copies + [copy]:
        done.wait()


def shards(momentum, grad, basis):
    rows, cols = momentum.shape
    n_col = lax.axis_size("col")
    n_row = lax.axis_size("row")
    n_z = n_row // 2
    per = rows // n_col
    scratch = [
        ((rows, cols), F32), ((rows, cols), BF16), ((cols, RANK), F32), ((rows, cols), BF16), ((rows, cols), BF16),
        ((cols, 2 * RANK), BF16), ((rows, RANK), F32), ((2 * RANK, rows), BF16), ((RANK, cols), F32), ((2 * RANK, cols), BF16),
        ((rows, RANK), F32), ((RANK, RANK), F32), ((RANK, RANK), F32), ((rows, 2 * RANK), F32),
        ((2, rows, RANK), F32), ((cols, RANK), F32),
        ((n_col, per, RANK), F32), ((n_col - 1, per, RANK), F32), ((n_col, per, RANK), F32),
        ((n_row, 8, RANK), F32), ((n_row - 1, 8, RANK), F32), ((n_row, 8, RANK), F32),
        ((n_col, 8, RANK), F32), ((n_col - 1, 8, RANK), F32), ((n_col, 8, RANK), F32),
    ]
    piece_scratch = []
    for _, width in pieces_of(cols):
        for count in (n_row, n_z, n_z, n_z - 1, n_row):
            piece_scratch.append(((count, 8, width), F32))
    sems = 6 + 4 * PIECES
    return pl.pallas_call(
        functools.partial(kernel, n_col, n_z),
        out_shape=(
            jax.ShapeDtypeStruct((rows, cols), F32),
            jax.ShapeDtypeStruct((2, rows, RANK), F32),
            jax.ShapeDtypeStruct((cols, RANK), F32),
        ),
        in_specs=[pl.BlockSpec(memory_space=pl.ANY)] * 3,
        out_specs=(pl.BlockSpec(memory_space=pl.ANY),) * 3,
        scratch_shapes=[pltpu.VMEM(s, t) for s, t in scratch]
        + [pltpu.SemaphoreType.DMA((11 + rows // TILE,)), pltpu.SemaphoreType.DMA((sems,)), pltpu.SemaphoreType.DMA((sems,))]
        + [pltpu.VMEM(s, t) for s, t in piece_scratch],
        compiler_params=pltpu.CompilerParams(
            collective_id=0, has_side_effects=True, vmem_limit_bytes=56 * 1024 * 1024
        ),
    )(momentum, grad, basis)


def solution(mesh):
    in_specs = (P("row", "col"), P("row", "col"), P("col", None))
    out_specs = (P("row", "col"), P(None, "row", None), P("col", None))
    return jax.shard_map(shards, mesh=mesh, in_specs=in_specs, out_specs=out_specs, check_vma=False)
```

```python
import functools
import math

import jax
import jax.numpy as jnp
from jax import lax
from jax.experimental import pallas as pl
from jax.experimental.pallas import tpu as pltpu
from jax.sharding import PartitionSpec as P

RANK = 128
TILE = 128
PANEL = 16
PIECES = 4
MESH = pl.DeviceIdType.MESH
HIGHEST = lax.Precision.HIGHEST
F32 = jnp.float32
BF16 = jnp.bfloat16
NN = (((1,), (0,)), ((), ()))
NT = (((1,), (1,)), ((), ()))
TN = (((0,), (0,)), ((), ()))


def dot(a, b, dims=NN):
    return lax.dot_general(a, b, dims, preferred_element_type=F32)


def exact(a, b, dims=NN):
    return lax.dot_general(a, b, dims, precision=HIGHEST, preferred_element_type=F32)


def split(x):
    high = x.astype(BF16)
    return high, (x - high.astype(F32)).astype(BF16)


def fold(a):
    return a[:, :RANK] + a[:, RANK:]


def tiles(total, size):
    return [(i, min(size, total - i)) for i in range(0, total, size)]


def pieces_of(cols):
    blocks = cols // 128
    edges = [blocks * i // PIECES * 128 for i in range(PIECES + 1)]
    return [(a, b - a) for a, b in zip(edges[:-1], edges[1:])]


def three(x):
    high, rest = x.astype(BF16), x
    rest = rest - high.astype(F32)
    middle = rest.astype(BF16)
    return high, middle, (rest - middle.astype(F32)).astype(BF16)


def inverse_cholesky(a_ref, first=0, last=RANK // PANEL):
    size = PANEL
    lane = lax.broadcasted_iota(jnp.int32, (size, RANK), 1)
    sub = lax.broadcasted_iota(jnp.int32, (size, RANK), 0)
    row_all = lax.broadcasted_iota(jnp.int32, (RANK, RANK), 0)
    lane_all = lax.broadcasted_iota(jnp.int32, (RANK, RANK), 1)

    def panel(k, carry):
        o = pl.multiple_of(k * size, size)
        v = a_ref[pl.ds(o, size), :]
        front = pltpu.roll(v, lax.rem(RANK - o, RANK), 1)
        cols = [jnp.broadcast_to(front[:, j : j + 1], (size, RANK)) for j in range(size)]
        inside = (lane >= o) & (lane < o + size)
        v = jnp.where(inside, jnp.where(lane == o + sub, 1.0, 0.0), v)
        pivots = []
        for j in range(size):
            d = cols[j][j : j + 1, :]
            pivots.append(d)
            d = jnp.broadcast_to(d, (8, RANK))
            r = pl.reciprocal(d, approx=True)
            r = r * (2.0 - d * r)
            r = r * (2.0 - d * r)
            m = jnp.where(sub > j, cols[j] * jnp.broadcast_to(r[:1], (size, RANK)), 0.0)
            v = v - m * jnp.broadcast_to(v[j : j + 1, :], (size, RANK))
            for l in range(j + 1, size):
                cols[l] = cols[l] - m * jnp.broadcast_to(cols[l][j : j + 1, :], (size, RANK))
        d = jnp.concatenate(pivots, axis=0)
        r = lax.rsqrt(d)
        v = v * (r * (1.5 - 0.5 * d * r * r))
        h, m, l = three(jnp.where(lane >= o + size, v, 0.0))
        high, middle, low = three(v)
        update = dot(
            jnp.concatenate([h, m, h, l, m, h], axis=0),
            jnp.concatenate([high, high, middle, high, middle, low], axis=0),
            TN,
        )
        old = a_ref[...]
        clear = (row_all >= o + size) & (lane_all >= o) & (lane_all < o + size)
        a_ref[...] = jnp.where(clear, 0.0, old) - update
        a_ref[pl.ds(o, size), :] = jnp.where(lane < o + size, v, 0.0)
        return carry

    lax.fori_loop(first, last, panel, 0)


def kernel(
    n_col, n_z, mom_ref, grad_ref, basis_ref, w, left_out, right_out,
    grads, base, wh, wl, b2, proj, pt2, rt, rt2, left, gram, full_gram, acc,
    c_src, c_rs, c_all, g_src, g_rs, g_all, h_src, h_rs, h_all,
    io, send, recv, *piece_refs,
):
    rows, cols = w.shape
    pieces = pieces_of(cols)
    parts = [piece_refs[i * 5 : i * 5 + 5] for i in range(PIECES)]
    row = lax.axis_index("row")
    me = lax.axis_index("col")
    z = row // 2
    core = lax.rem(row, 2)
    n_row = 2 * n_z
    total_rows = rows * n_row
    total_cols = cols * n_col
    per = rows // n_col
    at_col = lambda p: (row, p)
    at_row = lambda p: (p, me)
    at_z = lambda p: (p * 2 + core, me)
    partner = (z * 2 + 1 - core, me)
    home = pl.ds(pl.multiple_of(core * n_z, n_z), n_z)
    away = pl.ds(pl.multiple_of((1 - core) * n_z, n_z), n_z)
    row_tiles = tiles(rows, TILE)

    barrier = pltpu.get_barrier_semaphore()

    def far_first(n):
        return sorted(range(1, n), key=lambda s: -min(s, n - s))

    for s in far_first(n_row):
        pl.semaphore_signal(barrier, inc=1, device_id=at_row(lax.rem(row + s, n_row)), device_id_type=MESH)
    for s in far_first(n_col):
        pl.semaphore_signal(barrier, inc=1, device_id=at_col(lax.rem(me + s, n_col)), device_id_type=MESH)

    loads = [pltpu.make_async_copy(basis_ref, base, io.at[0])]
    for i, (o, size) in enumerate(row_tiles):
        loads.append(pltpu.make_async_copy(mom_ref.at[pl.ds(o, size), :], w.at[pl.ds(o, size), :], io.at[1 + 2 * i]))
        loads.append(pltpu.make_async_copy(grad_ref.at[pl.ds(o, size), :], grads.at[pl.ds(o, size), :], io.at[2 + 2 * i]))
    for load in loads:
        load.start()

    def remote(src, dst, sem, to):
        return pltpu.make_async_remote_copy(
            src_ref=src, dst_ref=dst, send_sem=send.at[sem], recv_sem=recv.at[sem],
            device_id=to, device_id_type=MESH,
        )

    def scatter(n, mine, at, src, rs, sem):
        def one(s, carry):
            p = lax.rem(mine + s, n)
            remote(src.at[p], rs.at[s - 1], sem, at(p)).start()
            return carry

        lax.fori_loop(1, n, one, 0)

    def gather(n, mine, at, src, rs, full, base_slot, sem):
        remote(rs, rs, sem, partner).wait_recv()
        total = src[mine]
        for s in range(n - 1):
            total = total + rs[s]
        slot = base_slot + mine
        full[slot] = total

        def one(s, carry):
            p = lax.rem(mine + s, n)
            remote(full.at[slot], full.at[slot], sem + 1, at(p)).start()
            return carry

        lax.fori_loop(1, n, one, 0)

    def finish(rs, sem):
        remote(rs, rs, sem + 1, partner).wait_recv()
        remote(rs, rs, sem, partner).wait_send()
        remote(rs, rs, sem + 1, partner).wait_send()

    piece_sem = lambda i: 6 + 4 * i

    def column_start(i, o, size, a):
        first, count = o // per, size // per
        c_src[pl.ds(first, count)] = a.reshape(count, per, RANK)
        for q in range(first, first + count):
            @pl.when(q != me)
            def _():
                s = lax.rem(q - me + n_col, n_col)
                remote(c_src.at[q], c_rs.at[s - 1], 0, at_col(q)).start()

    def row_sums():
        pt = proj[...].T
        h, l = split(pt)
        pt2[pl.ds(0, RANK), :] = h
        pt2[pl.ds(RANK, RANK), :] = l
        g_src[...] = exact(pt, pt, NT).reshape(n_row, 8, RANK)
        scatter(n_row, row, at_row, g_src, g_rs, 4)
        swaps = []

        def onward(i):
            st, half, total, rs, sx = parts[i]
            swaps[i].wait()
            total[...] = st[home] + half[...]
            scatter(n_z, z, at_z, total, rs, piece_sem(i) + 1)

        for i, (o, size) in enumerate(pieces):
            st, half, total, rs, sx = parts[i]
            a = dot(pt2[...], wh[:, pl.ds(o, size)]) + dot(pt2[...], wl[:, pl.ds(o, size)])
            st[...] = (a[:RANK] + a[RANK:]).reshape(n_row, 8, size)
            swap = remote(st.at[away], half, piece_sem(i), partner)
            swap.start()
            swaps.append(swap)
            if i:
                onward(i - 1)
        onward(PIECES - 1)

        def gather_piece(i):
            st, half, total, rs, sx = parts[i]
            gather(n_z, z, at_z, total, rs, sx, core * n_z, piece_sem(i) + 1)

        backs = []

        def give_back(i):
            st, half, total, rs, sx = parts[i]
            finish(rs, piece_sem(i) + 1)
            back = remote(sx.at[home], sx.at[home], piece_sem(i) + 3, partner)
            back.start()
            backs.append(back)

        gather(n_row, row, at_row, g_src, g_rs, g_all, 0, 4)
        gather_piece(0)
        gather_piece(1)
        finish(g_rs, 4)
        gram[...] = g_all[...].reshape(RANK, RANK)
        inverse_cholesky(gram, 0, 1)
        gather_piece(2)
        inverse_cholesky(gram, 1, 3)
        gather_piece(3)
        inverse_cholesky(gram, 3, 5)
        give_back(0)
        inverse_cholesky(gram, 5, 7)
        give_back(1)
        inverse_cholesky(gram, 7, 8)
        give_back(2)
        return backs, give_back

    def right_raw(backs, give_back, with_product):
        part = None
        for i, (o, size) in enumerate(pieces):
            if i == PIECES - 1:
                give_back(i)
            backs[i].wait()
            sx = parts[i][4]
            value = exact(gram[...], sx[...].reshape(RANK, size))
            rt[:, pl.ds(o, size)] = value
            h, l = split(value)
            rt2[pl.ds(0, RANK), pl.ds(o, size)] = h
            rt2[pl.ds(RANK, RANK), pl.ds(o, size)] = l
            mine = exact(value, value, NT)
            part = mine if part is None else part + mine
            if i == PIECES - 1:
                h_src[...] = part.reshape(n_col, 8, RANK)
                scatter(n_col, me, at_col, h_src, h_rs, 2)
            if with_product:
                for k, (q, height) in enumerate(row_tiles):
                    here = pl.ds(q, height)
                    wide = rt2[:, pl.ds(o, size)]
                    a = dot(wh[here, pl.ds(o, size)], wide, NT) + dot(wl[here, pl.ds(o, size)], wide, NT)
                    if i:
                        a = a + acc[here, :]
                    if i < PIECES - 1:
                        acc[here, :] = a
                    else:
                        column_start(k, q, height, fold(a))

    def set_left(index):
        for o, size in row_tiles:
            value = exact(proj[pl.ds(o, size), :], gram[...], NT)
            left[pl.ds(o, size), :] = value
            left_out[index, pl.ds(o, size), :] = value * F32(math.sqrt(total_rows))

    def deflate(o, size, again):
        h, l = split(left[pl.ds(o, size), :])
        hl = jnp.concatenate([h, l], axis=1)
        lh = jnp.concatenate([l, h], axis=1)
        for p, width in tiles(cols, 256):
            outer = dot(hl, rt2[:, pl.ds(p, width)]) + dot(lh, rt2[:, pl.ds(p, width)])
            value = w[pl.ds(o, size), pl.ds(p, width)] - 0.95 * outer
            w[pl.ds(o, size), pl.ds(p, width)] = value
            if again:
                h, l = split(value)
                wh[pl.ds(o, size), pl.ds(p, width)] = h
                wl[pl.ds(o, size), pl.ds(p, width)] = l

    loads[0].wait()
    h, l = split(base[...])
    b2[:, pl.ds(0, RANK)] = h
    b2[:, pl.ds(RANK, RANK)] = l
    for i, (o, size) in enumerate(row_tiles):
        here = pl.ds(o, size)
        loads[1 + 2 * i].wait()
        loads[2 + 2 * i].wait()
        for p, width in tiles(cols, 256):
            value = w[here, pl.ds(p, width)] + grads[here, pl.ds(p, width)].astype(F32)
            w[here, pl.ds(p, width)] = value
            h, l = split(value)
            wh[here, pl.ds(p, width)] = h
            wl[here, pl.ds(p, width)] = l
        a = fold(dot(wh[here, :], b2[...]) + dot(wl[here, :], b2[...]))
        if i == 0:
            pl.semaphore_wait(barrier, n_col + n_row - 2)
        column_start(i, o, size, a)
    gather(n_col, me, at_col, c_src, c_rs, c_all, 0, 0)
    finish(c_rs, 0)
    proj[...] = c_all[...].reshape(rows, RANK)

    sums = row_sums()
    right_raw(*sums, True)
    set_left(0)
    deflate(*row_tiles[0], True)
    gather(n_col, me, at_col, h_src, h_rs, h_all, 0, 2)
    deflate(*row_tiles[1], True)
    gather(n_col, me, at_col, c_src, c_rs, c_all, 0, 0)
    for o, size in row_tiles[2:]:
        deflate(o, size, True)
    finish(h_rs, 2)
    full_gram[...] = h_all[...].reshape(RANK, RANK)
    gram[...] = full_gram[...]
    inverse_cholesky(gram)
    finish(c_rs, 0)
    for o, size in row_tiles:
        here = pl.ds(o, size)
        value = c_all[pl.ds(o // per, size // per)].reshape(size, RANK) - 0.95 * exact(left[here, :], full_gram[...])
        proj[here, :] = exact(value, gram[...], NT)

    sums = row_sums()
    right_raw(*sums, False)
    set_left(1)
    for o, size in row_tiles[:2]:
        deflate(o, size, False)
    gather(n_col, me, at_col, h_src, h_rs, h_all, 0, 2)
    for o, size in row_tiles[2:]:
        deflate(o, size, False)
    finish(h_rs, 2)
    gram[...] = h_all[...].reshape(RANK, RANK)
    inverse_cholesky(gram)
    for o, size in tiles(cols, 128):
        value = exact(gram[...], rt[:, pl.ds(o, size)]) * F32(math.sqrt(total_cols))
        right_out[pl.ds(o, size), :] = value.T


def shards(momentum, grad, basis):
    rows, cols = momentum.shape
    n_col = lax.axis_size("col")
    n_row = lax.axis_size("row")
    n_z = n_row // 2
    per = rows // n_col
    scratch = [
        ((rows, cols), BF16), ((cols, RANK), F32), ((rows, cols), BF16), ((rows, cols), BF16),
        ((cols, 2 * RANK), BF16), ((rows, RANK), F32), ((2 * RANK, rows), BF16), ((RANK, cols), F32), ((2 * RANK, cols), BF16),
        ((rows, RANK), F32), ((RANK, RANK), F32), ((RANK, RANK), F32), ((rows, 2 * RANK), F32),
        ((n_col, per, RANK), F32), ((n_col - 1, per, RANK), F32), ((n_col, per, RANK), F32),
        ((n_row, 8, RANK), F32), ((n_row - 1, 8, RANK), F32), ((n_row, 8, RANK), F32),
        ((n_col, 8, RANK), F32), ((n_col - 1, 8, RANK), F32), ((n_col, 8, RANK), F32),
    ]
    piece_scratch = []
    for _, width in pieces_of(cols):
        for count in (n_row, n_z, n_z, n_z - 1, n_row):
            piece_scratch.append(((count, 8, width), F32))
    sems = 6 + 4 * PIECES
    return pl.pallas_call(
        functools.partial(kernel, n_col, n_z),
        out_shape=(
            pltpu.VMEM((rows, cols), F32),
            pltpu.VMEM((2, rows, RANK), F32),
            pltpu.VMEM((cols, RANK), F32),
        ),
        in_specs=[pl.BlockSpec(memory_space=pl.ANY)] * 3,
        out_specs=(pl.BlockSpec(memory_space=pltpu.VMEM),) * 3,
        scratch_shapes=[pltpu.VMEM(s, t) for s, t in scratch]
        + [pltpu.SemaphoreType.DMA((1 + 2 * (rows // TILE),)), pltpu.SemaphoreType.DMA((sems,)), pltpu.SemaphoreType.DMA((sems,))]
        + [pltpu.VMEM(s, t) for s, t in piece_scratch],
        compiler_params=pltpu.CompilerParams(
            collective_id=0, has_side_effects=True, vmem_limit_bytes=56 * 1024 * 1024
        ),
    )(momentum, grad, basis)


def solution(mesh):
    in_specs = (P("row", "col"), P("row", "col"), P("col", None))
    out_specs = (P("row", "col"), P(None, "row", None), P("col", None))
    return jax.shard_map(shards, mesh=mesh, in_specs=in_specs, out_specs=out_specs, check_vma=False)
```

```python
import functools
import math

import jax
import jax.numpy as jnp
from jax import lax
from jax.experimental import pallas as pl
from jax.experimental.pallas import tpu as pltpu
from jax.sharding import PartitionSpec as P

RANK = 128
TILE = 128
PANEL = 16
PIECES = 4
RELAYED = 4
MESH = pl.DeviceIdType.MESH
HIGHEST = lax.Precision.HIGHEST
F32 = jnp.float32
BF16 = jnp.bfloat16
NN = (((1,), (0,)), ((), ()))
NT = (((1,), (1,)), ((), ()))
TN = (((0,), (0,)), ((), ()))


def dot(a, b, dims=NN):
    return lax.dot_general(a, b, dims, preferred_element_type=F32)


def exact(a, b, dims=NN):
    return lax.dot_general(a, b, dims, precision=HIGHEST, preferred_element_type=F32)


def split(x):
    high = x.astype(BF16)
    return high, (x - high.astype(F32)).astype(BF16)


def fold(a):
    return a[:, :RANK] + a[:, RANK:]


def tiles(total, size):
    return [(i, min(size, total - i)) for i in range(0, total, size)]


def pieces_of(cols):
    blocks = cols // 128
    edges = [blocks * i // PIECES * 128 for i in range(PIECES + 1)]
    return [(a, b - a) for a, b in zip(edges[:-1], edges[1:])]


def three(x):
    high, rest = x.astype(BF16), x
    rest = rest - high.astype(F32)
    middle = rest.astype(BF16)
    return high, middle, (rest - middle.astype(F32)).astype(BF16)


def inverse_cholesky(a_ref, first=0, last=RANK // PANEL):
    size = PANEL
    lane = lax.broadcasted_iota(jnp.int32, (size, RANK), 1)
    sub = lax.broadcasted_iota(jnp.int32, (size, RANK), 0)
    row_all = lax.broadcasted_iota(jnp.int32, (RANK, RANK), 0)
    lane_all = lax.broadcasted_iota(jnp.int32, (RANK, RANK), 1)

    def panel(k, carry):
        o = pl.multiple_of(k * size, size)
        v = a_ref[pl.ds(o, size), :]
        front = pltpu.roll(v, lax.rem(RANK - o, RANK), 1)
        cols = [jnp.broadcast_to(front[:, j : j + 1], (size, RANK)) for j in range(size)]
        inside = (lane >= o) & (lane < o + size)
        v = jnp.where(inside, jnp.where(lane == o + sub, 1.0, 0.0), v)
        pivots = []
        for j in range(size):
            d = cols[j][j : j + 1, :]
            pivots.append(d)
            d = jnp.broadcast_to(d, (8, RANK))
            r = pl.reciprocal(d, approx=True)
            r = r * (2.0 - d * r)
            r = r * (2.0 - d * r)
            m = jnp.where(sub > j, cols[j] * jnp.broadcast_to(r[:1], (size, RANK)), 0.0)
            v = v - m * jnp.broadcast_to(v[j : j + 1, :], (size, RANK))
            for l in range(j + 1, size):
                cols[l] = cols[l] - m * jnp.broadcast_to(cols[l][j : j + 1, :], (size, RANK))
        d = jnp.concatenate(pivots, axis=0)
        r = lax.rsqrt(d)
        v = v * (r * (1.5 - 0.5 * d * r * r))
        h, m, l = three(jnp.where(lane >= o + size, v, 0.0))
        high, middle, low = three(v)
        update = dot(
            jnp.concatenate([h, m, h, l, m, h], axis=0),
            jnp.concatenate([high, high, middle, high, middle, low], axis=0),
            TN,
        )
        old = a_ref[...]
        clear = (row_all >= o + size) & (lane_all >= o) & (lane_all < o + size)
        a_ref[...] = jnp.where(clear, 0.0, old) - update
        a_ref[pl.ds(o, size), :] = jnp.where(lane < o + size, v, 0.0)
        return carry

    lax.fori_loop(first, last, panel, 0)


def kernel(
    n_col, n_z, mom_ref, grad_ref, basis_ref, w, left_out, right_out,
    grads, base, wh, wl, b2, proj, pt2, rt, rt2, left, gram, full_gram, acc,
    c_src, c_rs, c_all, g_src, g_rs, g_all, h_src, h_rs, h_all,
    io, send, recv, *piece_refs,
):
    rows, cols = w.shape
    pieces = pieces_of(cols)
    parts = [piece_refs[i * 6 : i * 6 + 6] for i in range(PIECES)]
    row = lax.axis_index("row")
    me = lax.axis_index("col")
    z = row // 2
    core = lax.rem(row, 2)
    n_row = 2 * n_z
    total_rows = rows * n_row
    total_cols = cols * n_col
    per = rows // n_col
    at_col = lambda p: (row, p)
    at_row = lambda p: (p, me)
    at_z = lambda p: (p * 2 + core, me)
    hop = lambda s: lax.rem(z + s, n_z)
    assert n_z == 8
    partner = (z * 2 + 1 - core, me)
    home = pl.ds(pl.multiple_of(core * n_z, n_z), n_z)
    away = pl.ds(pl.multiple_of((1 - core) * n_z, n_z), n_z)
    row_tiles = tiles(rows, TILE)
    order = list(range(RELAYED, PIECES)) + list(range(RELAYED))

    barrier = pltpu.get_barrier_semaphore()

    def far_first(n):
        return sorted(range(1, n), key=lambda s: -min(s, n - s))

    for s in far_first(n_row):
        pl.semaphore_signal(barrier, inc=1, device_id=at_row(lax.rem(row + s, n_row)), device_id_type=MESH)
    for s in far_first(n_col):
        pl.semaphore_signal(barrier, inc=1, device_id=at_col(lax.rem(me + s, n_col)), device_id_type=MESH)

    loads = [pltpu.make_async_copy(basis_ref, base, io.at[0])]
    for i, (o, size) in enumerate(row_tiles):
        loads.append(pltpu.make_async_copy(mom_ref.at[pl.ds(o, size), :], w.at[pl.ds(o, size), :], io.at[1 + 2 * i]))
        loads.append(pltpu.make_async_copy(grad_ref.at[pl.ds(o, size), :], grads.at[pl.ds(o, size), :], io.at[2 + 2 * i]))
    for load in loads:
        load.start()

    def remote(src, dst, sem, to):
        return pltpu.make_async_remote_copy(
            src_ref=src, dst_ref=dst, send_sem=send.at[sem], recv_sem=recv.at[sem],
            device_id=to, device_id_type=MESH,
        )

    def scatter(n, mine, at, src, rs, sem):
        def one(s, carry):
            p = lax.rem(mine + s, n)
            remote(src.at[p], rs.at[s - 1], sem, at(p)).start()
            return carry

        lax.fori_loop(1, n, one, 0)

    def gather(n, mine, at, src, rs, full, base_slot, sem):
        remote(rs, rs, sem, partner).wait_recv()
        total = src[mine]
        for s in range(n - 1):
            total = total + rs[s]
        slot = base_slot + mine
        full[slot] = total

        def one(s, carry):
            p = lax.rem(mine + s, n)
            remote(full.at[slot], full.at[slot], sem + 1, at(p)).start()
            return carry

        lax.fori_loop(1, n, one, 0)

    def chunks(ref, count, sem):
        some = ref.at[pl.ds(0, count)]
        return remote(some, some, sem, partner)

    def finish(rs, sem):
        remote(rs, rs, sem + 1, partner).wait_recv()
        remote(rs, rs, sem, partner).wait_send()
        remote(rs, rs, sem + 1, partner).wait_send()

    piece_sem = lambda i: 6 + 6 * i

    def column_start(i, o, size, a):
        first, count = o // per, size // per
        c_src[pl.ds(first, count)] = a.reshape(count, per, RANK)
        for q in range(first, first + count):
            @pl.when(q != me)
            def _():
                s = lax.rem(q - me + n_col, n_col)
                remote(c_src.at[q], c_rs.at[s - 1], 0, at_col(q)).start()

    def row_sums():
        pt = proj[...].T
        h, l = split(pt)
        pt2[pl.ds(0, RANK), :] = h
        pt2[pl.ds(RANK, RANK), :] = l
        g_src[...] = exact(pt, pt, NT).reshape(n_row, 8, RANK)
        scatter(n_row, row, at_row, g_src, g_rs, 4)
        swaps = []

        def onward(i):
            st, half, total, rs, sx, out = parts[i]
            swaps[i].wait()
            total[...] = st[home] + half[...]
            if i >= RELAYED:
                scatter(n_z, z, at_z, total, rs, piece_sem(i) + 1)
                return
            sem = piece_sem(i)
            remote(total.at[hop(5)], rs.at[4], sem + 4, at_z(hop(7))).start()
            remote(total.at[hop(3)], rs.at[5], sem + 4, at_z(hop(1))).start()
            remote(total.at[hop(4)], rs.at[6], sem + 4, at_z(hop(2 + 4 * core))).start()
            remote(total.at[hop(1)], rs.at[0], sem + 1, at_z(hop(1))).start()
            remote(total.at[hop(7)], rs.at[1], sem + 1, at_z(hop(7))).start()

        def relay(i):
            st, half, total, rs, sx, out = parts[i]
            sem = piece_sem(i)
            chunks(sx, 3, sem + 4).wait_recv()
            far = rs[6]
            out[0] = total[hop(2)] + rs[5] + jnp.where(core == 0, far, 0.0)
            out[1] = total[hop(6)] + rs[4] + jnp.where(core == 0, 0.0, far)
            remote(out.at[0], rs.at[2], sem + 1, at_z(hop(2))).start()
            remote(out.at[1], rs.at[3], sem + 1, at_z(hop(6))).start()

        for i, (o, size) in enumerate(pieces):
            st, half, total, rs, sx, out = parts[i]
            a = dot(pt2[...], wh[:, pl.ds(o, size)]) + dot(pt2[...], wl[:, pl.ds(o, size)])
            st[...] = (a[:RANK] + a[RANK:]).reshape(n_row, 8, size)
            swap = remote(st.at[away], half, piece_sem(i), partner)
            swap.start()
            swaps.append(swap)
            if i:
                onward(i - 1)
        onward(PIECES - 1)

        def gather_piece(i):
            st, half, total, rs, sx, out = parts[i]
            sem = piece_sem(i)
            if i >= RELAYED:
                gather(n_z, z, at_z, total, rs, sx, core * n_z, sem + 1)
                return
            chunks(sx, 4, sem + 1).wait_recv()
            mine = core * n_z + z
            sx[mine] = total[z] + ((rs[0] + rs[1]) + (rs[2] + rs[3]))
            for s in (2, 6):
                remote(sx.at[mine], sx.at[mine], sem + 5, at_z(hop(s))).start()
            for s in (1, 7):
                remote(sx.at[mine], sx.at[mine], sem + 2, at_z(hop(s))).start()

        def forward(i):
            sx = parts[i][4]
            sem = piece_sem(i)
            chunks(sx, 2, sem + 5).wait_recv()
            for source, to in ((6, 1), (2, 7), (6 + 4 * core, 2 + 4 * core)):
                slot = core * n_z + hop(source)
                remote(sx.at[slot], sx.at[slot], sem + 2, at_z(hop(to))).start()

        backs = {}

        def give_back(i):
            st, half, total, rs, sx, out = parts[i]
            sem = piece_sem(i)
            if i >= RELAYED:
                finish(rs, sem + 1)
            else:
                chunks(sx, 5, sem + 2).wait_recv()
                for part, count in ((4, 3), (1, 4), (5, 2), (2, 5)):
                    chunks(sx, count, sem + part).wait_send()
            back = remote(sx.at[home], sx.at[home], sem + 3, partner)
            back.start()
            backs[i] = back

        gather(n_row, row, at_row, g_src, g_rs, g_all, 0, 4)
        for i in range(RELAYED):
            relay(i)
        for i in range(RELAYED, PIECES):
            gather_piece(i)
        for i in range(RELAYED):
            gather_piece(i)
        finish(g_rs, 4)
        gram[...] = g_all[...].reshape(RANK, RANK)
        inverse_cholesky(gram, 0, 5)
        for i in range(RELAYED):
            forward(i)
        inverse_cholesky(gram, 5, 8)
        for i in order[:2]:
            give_back(i)
        return backs, give_back

    def right_raw(backs, give_back, with_product):
        part = None
        for n, i in enumerate(order):
            o, size = pieces[i]
            backs[i].wait()
            sx = parts[i][4]
            value = exact(gram[...], sx[...].reshape(RANK, size))
            rt[:, pl.ds(o, size)] = value
            h, l = split(value)
            rt2[pl.ds(0, RANK), pl.ds(o, size)] = h
            rt2[pl.ds(RANK, RANK), pl.ds(o, size)] = l
            mine = exact(value, value, NT)
            part = mine if part is None else part + mine
            if n == PIECES - 1:
                h_src[...] = part.reshape(n_col, 8, RANK)
                scatter(n_col, me, at_col, h_src, h_rs, 2)
            if with_product:
                for k, (q, height) in enumerate(row_tiles):
                    here = pl.ds(q, height)
                    wide = rt2[:, pl.ds(o, size)]
                    a = dot(wh[here, pl.ds(o, size)], wide, NT) + dot(wl[here, pl.ds(o, size)], wide, NT)
                    if n:
                        a = a + acc[here, :]
                    if n < PIECES - 1:
                        acc[here, :] = a
                    else:
                        column_start(k, q, height, fold(a))
            if n + 2 < PIECES:
                give_back(order[n + 2])

    def set_left(index):
        for o, size in row_tiles:
            value = exact(proj[pl.ds(o, size), :], gram[...], NT)
            left[pl.ds(o, size), :] = value
            left_out[index, pl.ds(o, size), :] = value * F32(math.sqrt(total_rows))

    def deflate(o, size, again):
        h, l = split(left[pl.ds(o, size), :])
        hl = jnp.concatenate([h, l], axis=1)
        lh = jnp.concatenate([l, h], axis=1)
        for p, width in tiles(cols, 256):
            outer = dot(hl, rt2[:, pl.ds(p, width)]) + dot(lh, rt2[:, pl.ds(p, width)])
            value = w[pl.ds(o, size), pl.ds(p, width)] - 0.95 * outer
            w[pl.ds(o, size), pl.ds(p, width)] = value
            if again:
                h, l = split(value)
                wh[pl.ds(o, size), pl.ds(p, width)] = h
                wl[pl.ds(o, size), pl.ds(p, width)] = l

    loads[0].wait()
    h, l = split(base[...])
    b2[:, pl.ds(0, RANK)] = h
    b2[:, pl.ds(RANK, RANK)] = l
    for i, (o, size) in enumerate(row_tiles):
        here = pl.ds(o, size)
        loads[1 + 2 * i].wait()
        loads[2 + 2 * i].wait()
        for p, width in tiles(cols, 256):
            value = w[here, pl.ds(p, width)] + grads[here, pl.ds(p, width)].astype(F32)
            w[here, pl.ds(p, width)] = value
            h, l = split(value)
            wh[here, pl.ds(p, width)] = h
            wl[here, pl.ds(p, width)] = l
        a = fold(dot(wh[here, :], b2[...]) + dot(wl[here, :], b2[...]))
        if i == 0:
            pl.semaphore_wait(barrier, n_col + n_row - 2)
        column_start(i, o, size, a)
    gather(n_col, me, at_col, c_src, c_rs, c_all, 0, 0)
    finish(c_rs, 0)
    proj[...] = c_all[...].reshape(rows, RANK)

    sums = row_sums()
    right_raw(*sums, True)
    set_left(0)
    deflate(*row_tiles[0], True)
    gather(n_col, me, at_col, h_src, h_rs, h_all, 0, 2)
    deflate(*row_tiles[1], True)
    gather(n_col, me, at_col, c_src, c_rs, c_all, 0, 0)
    for o, size in row_tiles[2:]:
        deflate(o, size, True)
    finish(h_rs, 2)
    full_gram[...] = h_all[...].reshape(RANK, RANK)
    gram[...] = full_gram[...]
    inverse_cholesky(gram)
    finish(c_rs, 0)
    for o, size in row_tiles:
        here = pl.ds(o, size)
        value = c_all[pl.ds(o // per, size // per)].reshape(size, RANK) - 0.95 * exact(left[here, :], full_gram[...])
        proj[here, :] = exact(value, gram[...], NT)

    sums = row_sums()
    right_raw(*sums, False)
    set_left(1)
    for o, size in row_tiles[:2]:
        deflate(o, size, False)
    gather(n_col, me, at_col, h_src, h_rs, h_all, 0, 2)
    for o, size in row_tiles[2:]:
        deflate(o, size, False)
    finish(h_rs, 2)
    gram[...] = h_all[...].reshape(RANK, RANK)
    inverse_cholesky(gram)
    for o, size in tiles(cols, 128):
        value = exact(gram[...], rt[:, pl.ds(o, size)]) * F32(math.sqrt(total_cols))
        right_out[pl.ds(o, size), :] = value.T


def shards(momentum, grad, basis):
    rows, cols = momentum.shape
    n_col = lax.axis_size("col")
    n_row = lax.axis_size("row")
    n_z = n_row // 2
    per = rows // n_col
    scratch = [
        ((rows, cols), BF16), ((cols, RANK), F32), ((rows, cols), BF16), ((rows, cols), BF16),
        ((cols, 2 * RANK), BF16), ((rows, RANK), F32), ((2 * RANK, rows), BF16), ((RANK, cols), F32), ((2 * RANK, cols), BF16),
        ((rows, RANK), F32), ((RANK, RANK), F32), ((RANK, RANK), F32), ((rows, 2 * RANK), F32),
        ((n_col, per, RANK), F32), ((n_col - 1, per, RANK), F32), ((n_col, per, RANK), F32),
        ((n_row, 8, RANK), F32), ((n_row - 1, 8, RANK), F32), ((n_row, 8, RANK), F32),
        ((n_col, 8, RANK), F32), ((n_col - 1, 8, RANK), F32), ((n_col, 8, RANK), F32),
    ]
    piece_scratch = []
    for _, width in pieces_of(cols):
        for count in (n_row, n_z, n_z, n_z - 1, n_row, 2):
            piece_scratch.append(((count, 8, width), F32))
    sems = 6 + 6 * PIECES
    return pl.pallas_call(
        functools.partial(kernel, n_col, n_z),
        out_shape=(
            pltpu.VMEM((rows, cols), F32),
            pltpu.VMEM((2, rows, RANK), F32),
            pltpu.VMEM((cols, RANK), F32),
        ),
        in_specs=[pl.BlockSpec(memory_space=pl.ANY)] * 3,
        out_specs=(pl.BlockSpec(memory_space=pltpu.VMEM),) * 3,
        scratch_shapes=[pltpu.VMEM(s, t) for s, t in scratch]
        + [pltpu.SemaphoreType.DMA((1 + 2 * (rows // TILE),)), pltpu.SemaphoreType.DMA((sems,)), pltpu.SemaphoreType.DMA((sems,))]
        + [pltpu.VMEM(s, t) for s, t in piece_scratch],
        compiler_params=pltpu.CompilerParams(
            collective_id=0, has_side_effects=True, vmem_limit_bytes=56 * 1024 * 1024
        ),
    )(momentum, grad, basis)


def solution(mesh):
    in_specs = (P("row", "col"), P("row", "col"), P("col", None))
    out_specs = (P("row", "col"), P(None, "row", None), P("col", None))
    return jax.shard_map(shards, mesh=mesh, in_specs=in_specs, out_specs=out_specs, check_vma=False)
```

```python
import functools
import math

import jax
import jax.numpy as jnp
from jax import lax
from jax.experimental import pallas as pl
from jax.experimental.pallas import tpu as pltpu
from jax.sharding import PartitionSpec as P

RANK = 128
TILE = 128
PANEL = 16
PIECES = 3
MESH = pl.DeviceIdType.MESH
HIGHEST = lax.Precision.HIGHEST
F32 = jnp.float32
BF16 = jnp.bfloat16
NN = (((1,), (0,)), ((), ()))
NT = (((1,), (1,)), ((), ()))
TN = (((0,), (0,)), ((), ()))


def dot(a, b, dims=NN):
    return lax.dot_general(a, b, dims, preferred_element_type=F32)


def exact(a, b, dims=NN):
    return lax.dot_general(a, b, dims, precision=HIGHEST, preferred_element_type=F32)


def split(x):
    high = x.astype(BF16)
    return high, (x - high.astype(F32)).astype(BF16)


def fold(a):
    return a[:, :RANK] + a[:, RANK:]


def tiles(total, size):
    return [(i, min(size, total - i)) for i in range(0, total, size)]


def pieces_of(cols):
    blocks = cols // 128
    edges = [blocks * i // PIECES * 128 for i in range(PIECES + 1)]
    return [(a, b - a) for a, b in zip(edges[:-1], edges[1:])]


def three(x):
    high, rest = x.astype(BF16), x
    rest = rest - high.astype(F32)
    middle = rest.astype(BF16)
    return high, middle, (rest - middle.astype(F32)).astype(BF16)


def inverse_cholesky(a_ref, first=0, last=RANK // PANEL, unrolled=False):
    size = PANEL
    lane = lax.broadcasted_iota(jnp.int32, (size, RANK), 1)
    sub = lax.broadcasted_iota(jnp.int32, (size, RANK), 0)
    row_all = lax.broadcasted_iota(jnp.int32, (RANK, RANK), 0)
    lane_all = lax.broadcasted_iota(jnp.int32, (RANK, RANK), 1)

    def panel(k, carry):
        o = k * size if unrolled else pl.multiple_of(k * size, size)
        v = a_ref[pl.ds(o, size), :]
        front = v[:, o : o + size] if unrolled else pltpu.roll(v, lax.rem(RANK - o, RANK), 1)
        cols = [jnp.broadcast_to(front[:, j : j + 1], (size, RANK)) for j in range(size)]
        inside = (lane >= o) & (lane < o + size)
        v = jnp.where(inside, jnp.where(lane == o + sub, 1.0, 0.0), v)
        pivots = []
        for j in range(size):
            d = cols[j][j : j + 1, :]
            pivots.append(d)
            d = jnp.broadcast_to(d, (8, RANK))
            r = pl.reciprocal(d, approx=True)
            r = r * (2.0 - d * r)
            m = jnp.where(sub > j, cols[j] * jnp.broadcast_to(r[:1], (size, RANK)), 0.0)
            v = v - m * jnp.broadcast_to(v[j : j + 1, :], (size, RANK))
            for l in range(j + 1, size):
                cols[l] = cols[l] - m * jnp.broadcast_to(cols[l][j : j + 1, :], (size, RANK))
        d = jnp.concatenate(pivots, axis=0)
        r = lax.rsqrt(d)
        v = v * (r * (1.5 - 0.5 * d * r * r))
        if unrolled and o + size == RANK:
            a_ref[pl.ds(o, size), :] = v
            return carry
        h, m, l = three(jnp.where(lane >= o + size, v, 0.0))
        high, middle, low = three(v)
        update = dot(
            jnp.concatenate([h, m, h, l, m, h], axis=0),
            jnp.concatenate([high, high, middle, high, middle, low], axis=0),
            TN,
        )
        clear = (row_all >= o + size) & (lane_all >= o) & (lane_all < o + size)
        value = jnp.where(clear, 0.0, a_ref[...]) - update
        if unrolled:
            a_ref[pl.ds(o + size, RANK - o - size), :] = value[o + size :]
        else:
            a_ref[...] = value
        a_ref[pl.ds(o, size), :] = jnp.where(lane < o + size, v, 0.0)
        return carry

    if unrolled:
        for k in range(first, last):
            panel(k, 0)
    else:
        lax.fori_loop(first, last, panel, 0)


def kernel(
    n_col, n_z, mom_ref, grad_ref, basis_ref, w, left_out, right_out,
    grads, base, wh, wl, b2, proj, pt2, rt, rt2, left, gram, full_gram, acc,
    c_src, c_rs, c_all, g_src, g_rs, g_all, h_src, h_rs, h_all,
    io, send, recv, *piece_refs,
):
    rows, cols = w.shape
    pieces = pieces_of(cols)
    parts = [piece_refs[i * 6 : i * 6 + 6] for i in range(PIECES)]
    row = lax.axis_index("row")
    me = lax.axis_index("col")
    z = row // 2
    core = lax.rem(row, 2)
    n_row = 2 * n_z
    total_rows = rows * n_row
    total_cols = cols * n_col
    per = rows // n_col
    wide = int(math.sqrt(n_col))
    assert wide * wide == n_col
    y, x = me // wide, lax.rem(me, wide)
    near = lambda s, n: min(s, n - s)
    col_peers = [
        (dy * wide + dx - 1, lax.rem(y + dy, wide) * wide + lax.rem(x + dx, wide))
        for dy, dx in sorted(
            [(i, j) for i in range(wide) for j in range(wide) if i or j],
            key=lambda d: -near(d[0], wide) - near(d[1], wide),
        )
    ]
    row_peers = [
        (dz * 2 + dc - 1, lax.rem(z + dz, n_z) * 2 + lax.rem(core + dc, 2))
        for dz, dc in sorted(
            [(i, j) for i in range(n_z) for j in range(2) if i or j], key=lambda d: -near(d[0], n_z)
        )
    ]
    at = lambda group, p: (row, p) if group is col_peers else (p, me)
    at_z = lambda p: (p * 2 + core, me)
    hop = lambda s: lax.rem(z + s, n_z)
    assert n_z == 8
    partner = (z * 2 + 1 - core, me)
    home = pl.ds(pl.multiple_of(core * n_z, n_z), n_z)
    away = pl.ds(pl.multiple_of((1 - core) * n_z, n_z), n_z)
    row_tiles = tiles(rows, TILE)
    order = list(range(PIECES))

    barrier = pltpu.get_barrier_semaphore()

    for group in (row_peers, col_peers):
        for slot, p in group:
            pl.semaphore_signal(barrier, inc=1, device_id=at(group, p), device_id_type=MESH)

    loads = [pltpu.make_async_copy(basis_ref, base, io.at[0])]
    for i, (o, size) in enumerate(row_tiles):
        loads.append(pltpu.make_async_copy(mom_ref.at[pl.ds(o, size), :], w.at[pl.ds(o, size), :], io.at[1 + 2 * i]))
        loads.append(pltpu.make_async_copy(grad_ref.at[pl.ds(o, size), :], grads.at[pl.ds(o, size), :], io.at[2 + 2 * i]))
    for load in loads:
        load.start()

    def remote(src, dst, sem, to):
        return pltpu.make_async_remote_copy(
            src_ref=src, dst_ref=dst, send_sem=send.at[sem], recv_sem=recv.at[sem],
            device_id=to, device_id_type=MESH,
        )

    def scatter(group, src, rs, sem):
        for slot, p in group:
            remote(src.at[p], rs.at[slot], sem, at(group, p)).start()

    def gather(group, src, rs, full, sem):
        mine = me if group is col_peers else row
        remote(rs, rs, sem, partner).wait_recv()
        total = src[mine]
        for s in range(rs.shape[0]):
            total = total + rs[s]
        full[mine] = total
        for slot, p in group:
            remote(full.at[mine], full.at[mine], sem + 1, at(group, p)).start()

    def chunks(ref, count, sem):
        some = ref.at[pl.ds(0, count)]
        return remote(some, some, sem, partner)

    def finish(rs, sem):
        remote(rs, rs, sem + 1, partner).wait_recv()
        remote(rs, rs, sem, partner).wait_send()
        remote(rs, rs, sem + 1, partner).wait_send()

    piece_sem = lambda i: 6 + 6 * i

    def column_start(i, o, size, a):
        first, count = o // per, size // per
        c_src[pl.ds(first, count)] = a.reshape(count, per, RANK)
        for q in range(first, first + count):
            @pl.when(q != me)
            def _():
                dy = lax.rem(q // wide + wide - y, wide)
                dx = lax.rem(q % wide + wide - x, wide)
                remote(c_src.at[q], c_rs.at[dy * wide + dx - 1], 0, (row, q)).start()

    def row_sums():
        pt = proj[...].T
        h, l = split(pt)
        pt2[pl.ds(0, RANK), :] = h
        pt2[pl.ds(RANK, RANK), :] = l
        g_src[...] = exact(pt, pt, NT).reshape(n_row, 8, RANK)
        scatter(row_peers, g_src, g_rs, 4)
        swaps = []

        def onward(i):
            st, half, total, rs, sx, out = parts[i]
            swaps[i].wait()
            total[...] = st[home] + half[...]
            sem = piece_sem(i)
            remote(total.at[hop(5)], rs.at[4], sem + 4, at_z(hop(7))).start()
            remote(total.at[hop(3)], rs.at[5], sem + 4, at_z(hop(1))).start()
            remote(total.at[hop(4)], rs.at[6], sem + 4, at_z(hop(2 + 4 * core))).start()
            remote(total.at[hop(1)], rs.at[0], sem + 1, at_z(hop(1))).start()
            remote(total.at[hop(7)], rs.at[1], sem + 1, at_z(hop(7))).start()

        def relay(i):
            st, half, total, rs, sx, out = parts[i]
            sem = piece_sem(i)
            chunks(sx, 3, sem + 4).wait_recv()
            far = rs[6]
            out[0] = total[hop(2)] + rs[5] + jnp.where(core == 0, far, 0.0)
            out[1] = total[hop(6)] + rs[4] + jnp.where(core == 0, 0.0, far)
            remote(out.at[0], rs.at[2], sem + 1, at_z(hop(2))).start()
            remote(out.at[1], rs.at[3], sem + 1, at_z(hop(6))).start()

        for i, (o, size) in enumerate(pieces):
            st, half, total, rs, sx, out = parts[i]
            a = dot(pt2[...], wh[:, pl.ds(o, size)]) + dot(pt2[...], wl[:, pl.ds(o, size)])
            st[...] = (a[:RANK] + a[RANK:]).reshape(n_row, 8, size)
            swap = remote(st.at[away], half, piece_sem(i), partner)
            swap.start()
            swaps.append(swap)
            if i:
                onward(i - 1)
        onward(PIECES - 1)

        def gather_piece(i):
            st, half, total, rs, sx, out = parts[i]
            sem = piece_sem(i)
            chunks(sx, 4, sem + 1).wait_recv()
            mine = core * n_z + z
            sx[mine] = total[z] + ((rs[0] + rs[1]) + (rs[2] + rs[3]))
            for s in (2, 6):
                remote(sx.at[mine], sx.at[mine], sem + 5, at_z(hop(s))).start()
            for s in (1, 7):
                remote(sx.at[mine], sx.at[mine], sem + 2, at_z(hop(s))).start()

        def forward(i):
            sx = parts[i][4]
            sem = piece_sem(i)
            chunks(sx, 2, sem + 5).wait_recv()
            for source, to in ((6, 1), (2, 7), (6 + 4 * core, 2 + 4 * core)):
                slot = core * n_z + hop(source)
                remote(sx.at[slot], sx.at[slot], sem + 2, at_z(hop(to))).start()

        backs = {}

        def give_back(i):
            st, half, total, rs, sx, out = parts[i]
            sem = piece_sem(i)
            chunks(sx, 5, sem + 2).wait_recv()
            for part, count in ((4, 3), (1, 4), (5, 2), (2, 5)):
                chunks(sx, count, sem + part).wait_send()
            back = remote(sx.at[home], sx.at[home], sem + 3, partner)
            back.start()
            backs[i] = back

        gather(row_peers, g_src, g_rs, g_all, 4)
        for i in range(PIECES):
            relay(i)
        for i in range(PIECES):
            gather_piece(i)
        finish(g_rs, 4)
        gram[...] = g_all[...].reshape(RANK, RANK)
        inverse_cholesky(gram, 0, 5)
        for i in range(PIECES):
            forward(i)
        inverse_cholesky(gram, 5, 8)
        for i in order[:2]:
            give_back(i)
        return backs, give_back

    def right_raw(backs, give_back, with_product):
        part = None
        for n, i in enumerate(order):
            o, size = pieces[i]
            backs[i].wait()
            sx = parts[i][4]
            value = exact(gram[...], sx[...].reshape(RANK, size))
            rt[:, pl.ds(o, size)] = value
            h, l = split(value)
            rt2[pl.ds(0, RANK), pl.ds(o, size)] = h
            rt2[pl.ds(RANK, RANK), pl.ds(o, size)] = l
            mine = exact(value, value, NT)
            part = mine if part is None else part + mine
            if n == PIECES - 1:
                h_src[...] = part.reshape(n_col, 8, RANK)
                scatter(col_peers, h_src, h_rs, 2)
            if with_product:
                for k, (q, height) in enumerate(row_tiles):
                    here = pl.ds(q, height)
                    wide = rt2[:, pl.ds(o, size)]
                    a = dot(wh[here, pl.ds(o, size)], wide, NT) + dot(wl[here, pl.ds(o, size)], wide, NT)
                    if n:
                        a = a + acc[here, :]
                    if n < PIECES - 1:
                        acc[here, :] = a
                    else:
                        column_start(k, q, height, fold(a))
            if n + 2 < PIECES:
                give_back(order[n + 2])

    def set_left(index):
        for o, size in row_tiles:
            value = exact(proj[pl.ds(o, size), :], gram[...], NT)
            left[pl.ds(o, size), :] = value
            left_out[index, pl.ds(o, size), :] = value * F32(math.sqrt(total_rows))

    def deflate(o, size, again):
        h, l = split(left[pl.ds(o, size), :])
        hl = jnp.concatenate([h, l], axis=1)
        lh = jnp.concatenate([l, h], axis=1)
        for p, width in tiles(cols, 256):
            outer = dot(hl, rt2[:, pl.ds(p, width)]) + dot(lh, rt2[:, pl.ds(p, width)])
            value = w[pl.ds(o, size), pl.ds(p, width)] - 0.95 * outer
            w[pl.ds(o, size), pl.ds(p, width)] = value
            if again:
                h, l = split(value)
                wh[pl.ds(o, size), pl.ds(p, width)] = h
                wl[pl.ds(o, size), pl.ds(p, width)] = l

    loads[0].wait()
    h, l = split(base[...])
    b2[:, pl.ds(0, RANK)] = h
    b2[:, pl.ds(RANK, RANK)] = l
    for i, (o, size) in enumerate(row_tiles):
        here = pl.ds(o, size)
        loads[1 + 2 * i].wait()
        loads[2 + 2 * i].wait()
        for p, width in tiles(cols, 256):
            value = w[here, pl.ds(p, width)] + grads[here, pl.ds(p, width)].astype(F32)
            w[here, pl.ds(p, width)] = value
            h, l = split(value)
            wh[here, pl.ds(p, width)] = h
            wl[here, pl.ds(p, width)] = l
        a = fold(dot(wh[here, :], b2[...]) + dot(wl[here, :], b2[...]))
        if i == 0:
            pl.semaphore_wait(barrier, n_col + n_row - 2)
        column_start(i, o, size, a)
    gather(col_peers, c_src, c_rs, c_all, 0)
    finish(c_rs, 0)
    proj[...] = c_all[...].reshape(rows, RANK)

    sums = row_sums()
    right_raw(*sums, True)
    set_left(0)
    deflate(*row_tiles[0], True)
    gather(col_peers, h_src, h_rs, h_all, 2)
    deflate(*row_tiles[1], True)
    gather(col_peers, c_src, c_rs, c_all, 0)
    for o, size in row_tiles[2:]:
        deflate(o, size, True)
    finish(h_rs, 2)
    full_gram[...] = h_all[...].reshape(RANK, RANK)
    gram[...] = full_gram[...]
    inverse_cholesky(gram, unrolled=True)
    finish(c_rs, 0)
    for o, size in row_tiles:
        here = pl.ds(o, size)
        value = c_all[pl.ds(o // per, size // per)].reshape(size, RANK) - 0.95 * exact(left[here, :], full_gram[...])
        proj[here, :] = exact(value, gram[...], NT)

    sums = row_sums()
    right_raw(*sums, False)
    set_left(1)
    for o, size in row_tiles[:2]:
        deflate(o, size, False)
    gather(col_peers, h_src, h_rs, h_all, 2)
    for o, size in row_tiles[2:]:
        deflate(o, size, False)
    finish(h_rs, 2)
    gram[...] = h_all[...].reshape(RANK, RANK)
    inverse_cholesky(gram, unrolled=True)
    for o, size in tiles(cols, 128):
        value = exact(gram[...], rt[:, pl.ds(o, size)]) * F32(math.sqrt(total_cols))
        right_out[pl.ds(o, size), :] = value.T


def shards(momentum, grad, basis):
    rows, cols = momentum.shape
    n_col = lax.axis_size("col")
    n_row = lax.axis_size("row")
    n_z = n_row // 2
    per = rows // n_col
    scratch = [
        ((rows, cols), BF16), ((cols, RANK), F32), ((rows, cols), BF16), ((rows, cols), BF16),
        ((cols, 2 * RANK), BF16), ((rows, RANK), F32), ((2 * RANK, rows), BF16), ((RANK, cols), F32), ((2 * RANK, cols), BF16),
        ((rows, RANK), F32), ((RANK, RANK), F32), ((RANK, RANK), F32), ((rows, 2 * RANK), F32),
        ((n_col, per, RANK), F32), ((n_col - 1, per, RANK), F32), ((n_col, per, RANK), F32),
        ((n_row, 8, RANK), F32), ((n_row - 1, 8, RANK), F32), ((n_row, 8, RANK), F32),
        ((n_col, 8, RANK), F32), ((n_col - 1, 8, RANK), F32), ((n_col, 8, RANK), F32),
    ]
    piece_scratch = []
    for _, width in pieces_of(cols):
        for count in (n_row, n_z, n_z, n_z - 1, n_row, 2):
            piece_scratch.append(((count, 8, width), F32))
    sems = 6 + 6 * PIECES
    return pl.pallas_call(
        functools.partial(kernel, n_col, n_z),
        out_shape=(
            pltpu.VMEM((rows, cols), F32),
            pltpu.VMEM((2, rows, RANK), F32),
            pltpu.VMEM((cols, RANK), F32),
        ),
        in_specs=[pl.BlockSpec(memory_space=pl.ANY)] * 3,
        out_specs=(pl.BlockSpec(memory_space=pltpu.VMEM),) * 3,
        scratch_shapes=[pltpu.VMEM(s, t) for s, t in scratch]
        + [pltpu.SemaphoreType.DMA((1 + 2 * (rows // TILE),)), pltpu.SemaphoreType.DMA((sems,)), pltpu.SemaphoreType.DMA((sems,))]
        + [pltpu.VMEM(s, t) for s, t in piece_scratch],
        compiler_params=pltpu.CompilerParams(
            collective_id=0, has_side_effects=True, vmem_limit_bytes=56 * 1024 * 1024
        ),
    )(momentum, grad, basis)


def solution(mesh):
    in_specs = (P("row", "col"), P("row", "col"), P("col", None))
    out_specs = (P("row", "col"), P(None, "row", None), P("col", None))
    return jax.shard_map(shards, mesh=mesh, in_specs=in_specs, out_specs=out_specs, check_vma=False)
```
